512 devices in a mesh: row: 16 (over z_lo, y), col: 32 (over x, z_hi, core).
Axes of the slice: x: 4, y: 8, z: 8 (z_hi: 4, z_lo: 2; z = z_hi * 2 + z_lo), core: 2. Of those that a mesh axis runs over, the one named last changes fastest.
Arguments:
- stored: float32 [16, 32, 8, 128, 128], P('row', 'col'), as said below
- pair_lists: int32 [16, 32, 3, 3, 128], P('row', 'col'), may hold values from 0 to 16, as said below
Outputs:
- square_tiles: float32 [16, 32, 8, 128, 128], P('row', 'col')
The draws below stay inside these ranges and needn't reach their ends.
Inputs may be any that keep to these rules, and one draw needn't show every extreme that they name: stored[r, 2 j] holds the upper-triangle tiles of panel (r, j) and is zero where r > j; stored[r, 2 j + 1] equals stored[j, 2 r]. With j = c // 2 and k = (r + j + s) mod 16, an entry (x, y, t) of pair_lists[r, c, s] is real when t < 16: then x lies in the first 8 slots of panel_list(r, k) if r < k and in the last 8 if r > k, y likewise for panel_list(k, j). Other entries have all three indices equal to 16 and follow all real ones of their list. Some list has 128 real entries.
All inputs are finite; a program needn't handle non-finite values.
Results may differ from the reference program's by a relative error of at most 0.0003.
Values sent between devices are 32-bit elements; how exact they have to be, the bound alone decides.
No kernel may reach another device: no remote copies, remote signals or barrier semaphores. Data moves between devices by JAX's collectives and lax.ppermute only.
A program may use at most 64 MiB of HBM per device.

```python
import jax
import jax.numpy as jnp
from jax import lax

BS = 128
SU = 8
NPAIR = 128
STEPS = 3
GRID = 16


def draw_stored(key, part):
    key = jax.random.fold_in(key, 11)
    shape = (GRID, GRID, SU, BS, BS)
    base = 0.2 * jax.random.normal(key, shape, jnp.float32)
    first = jnp.arange(GRID)[:, None]
    second = jnp.arange(GRID)[None, :]
    upper = base * (first <= second).astype(jnp.float32)[:, :, None, None, None]
    mirror = jnp.swapaxes(base, 0, 1) * (second <= first).astype(jnp.float32)[:, :, None, None, None]
    return jnp.stack([upper, mirror], axis=2).reshape(GRID, 2 * GRID, SU, BS, BS)


def draw_pair_lists(key, part):
    key = jax.random.fold_in(key, 23)
    heads = (GRID, 2 * GRID, STEPS)
    shape = (GRID, 2 * GRID, STEPS, NPAIR)
    draws = jax.random.randint(jax.random.fold_in(key, 1), heads, 1, NPAIR + 1)
    counts = draws * draws // NPAIR
    chosen = jax.random.randint(jax.random.fold_in(key, 2), (), 0, GRID * 2 * GRID * STEPS)
    flat = jnp.arange(GRID * 2 * GRID * STEPS, dtype=jnp.int32).reshape(heads)
    counts = jnp.where(flat == chosen, NPAIR, counts)
    r_idx = jnp.arange(GRID, dtype=jnp.int32)[:, None, None]
    c_idx = jnp.arange(2 * GRID, dtype=jnp.int32)[None, :, None]
    s_idx = jnp.arange(STEPS, dtype=jnp.int32)[None, None, :]
    j_idx = c_idx // 2
    k_idx = (r_idx + j_idx + s_idx) % GRID

    def window(first, second):
        start = jnp.where(first > second, SU, 0)
        width = jnp.where(first == second, 2 * SU, SU)
        return (start[..., None], width[..., None])
    start_a, width_a = window(r_idx, k_idx)
    start_b, width_b = window(k_idx, j_idx)
    raw_a = jax.random.randint(jax.random.fold_in(key, 3), shape, 0, 1 << 20)
    raw_b = jax.random.randint(jax.random.fold_in(key, 4), shape, 0, 1 << 20)
    first_idx = start_a + raw_a % width_a
    second_idx = start_b + raw_b % width_b
    target = jax.random.randint(jax.random.fold_in(key, 5), shape, 0, 2 * SU)
    valid = jnp.arange(NPAIR, dtype=jnp.int32)[None, None, None, :] < counts[..., None]
    padding = 2 * SU
    first_idx = jnp.where(valid, first_idx, padding)
    second_idx = jnp.where(valid, second_idx, padding)
    target = jnp.where(valid, target, padding)
    return jnp.stack([first_idx, second_idx, target], axis=3).astype(jnp.int32)


def setup_inputs(seed: int = 0) -> dict:
    splits = jax.random.split(jax.random.key(seed), 3)
    return {
        "stored": draw_stored(jax.random.fold_in(splits[2], 71), 0),
        "pair_lists": draw_pair_lists(jax.random.fold_in(splits[2], 71), 0),
    }


def tile_block(left, right, entry, limit):
    first_idx = jnp.minimum(entry[0], limit - 1)
    second_idx = jnp.minimum(entry[1], limit - 1)
    a_tiles = jnp.take(left, first_idx, axis=0)
    b_tiles = jnp.take(right, second_idx, axis=0)
    blocks = jnp.einsum("pij,pjk->pik", a_tiles, b_tiles, precision=lax.Precision.HIGHEST)
    target = (entry[2][None, :] == jnp.arange(limit, dtype=jnp.int32)[:, None]).astype(jnp.float32)
    return jnp.einsum("tp,pik->tik", target, blocks, precision=lax.Precision.HIGHEST)


def panel_of(stored, first, second):
    upper = stored[first, 2 * second]
    mirror = stored[first, 2 * second + 1]
    return jnp.concatenate([upper, jnp.swapaxes(mirror, 1, 2)], axis=0)


def reference(stored, pair_lists):
    limit = 2 * SU

    def one_panel(index):
        r_idx = (index // GRID).astype(jnp.int32)
        j_idx = (index % GRID).astype(jnp.int32)
        total = jnp.zeros((limit, BS, BS), jnp.float32)
        for core in range(2):
            for step in range(STEPS):
                k_idx = ((r_idx + j_idx + step) % GRID).astype(jnp.int32)
                left = panel_of(stored, r_idx, k_idx)
                right = panel_of(stored, k_idx, j_idx)
                entry = pair_lists[r_idx, 2 * j_idx + core, step]
                total = total + tile_block(left, right, entry, limit)
        return total

    whole = lax.map(one_panel, jnp.arange(GRID * GRID, dtype=jnp.int32))
    whole = whole.reshape(GRID, GRID, 2, SU, BS, BS)
    return whole.reshape(GRID, 2 * GRID, SU, BS, BS)
```

```python
import jax
import jax.numpy as jnp
from jax import lax
from jax.experimental import pallas as pl
from jax.experimental.pallas import tpu as pltpu
from jax.sharding import PartitionSpec as P

STEPS = 3
GRID = 16
SU = 8
BS = 128
NPAIR = 128
AXES = ("row", "col")


def device(r, j, core):
    return (r * GRID + j) * 2 + core


def data_core(a, b):
    return 0 if a <= b else 1


def left_plan(r, j, phase):
    low = r < 8
    if phase == 0:
        step = 0 if low else 2
    elif phase == 1:
        step = 2 if low else 0
    else:
        step = 1
    if phase < 2:
        return step, (r, (r + j + step) % GRID)
    return step, (r, (j + 1) % GRID if low else (j - 1) % GRID)


def right_order(j):
    m = j % 8
    if m <= 2:
        return (0, 1, 2)
    if m in (3, 7):
        return (1, 0, 2)
    return (2, 1, 0)


def right_plan(r, j, phase):
    m = j % 8
    if phase == 0:
        step = right_order(j)[0]
        return step, ((r + j + step) % GRID, j)
    if m in (3, 7):
        step = (2 if r % 2 == 0 else 0) if phase == 1 else (0 if r % 2 == 0 else 2)
        return step, ((r + 1) % GRID if step == 2 else (r - 1) % GRID, j)
    return right_order(j)[phase], ((r + 1) % GRID if m <= 2 else (r - 1) % GRID, j)


def route(phase):
    pairs = []
    for r in range(GRID):
        for j in range(GRID):
            pairs.append((device(*left_plan(r, j, phase)[1], 0), device(r, j, 0)))
            pairs.append((device(*right_plan(r, j, phase)[1], 1), device(r, j, 1)))
    return pairs


def init_route():
    out = []
    for a in range(GRID):
        for b in range(GRID):
            core = data_core(a, b)
            out.append((device(a, b, core), device(a, b, 1 - core)))
    return out


def swap_route():
    return [(d, d ^ 1) for d in range(2 * GRID * GRID)]


def bucket_kernel(core_ref, own_ref, other_ref, codes_ref, counts_ref):
    core = core_ref[0]
    for step in range(STEPS):
        for t in range(SU + 1):
            counts_ref[step, t] = 0
        for ref in (own_ref, other_ref):

            def more(i, ref=ref, step=step):
                return jnp.logical_and(i < NPAIR, ref[step, 2, jnp.minimum(i, NPAIR - 1)] < 2 * SU)

            def put(i, ref=ref, step=step):
                x = jnp.minimum(ref[step, 0, i], 2 * SU - 1)
                y = jnp.minimum(ref[step, 1, i], 2 * SU - 1)
                t = ref[step, 2, i] - core * SU
                mine = jnp.logical_and(t >= 0, t < SU)
                slot = jnp.where(mine, t, SU)
                n = counts_ref[step, slot]
                codes_ref[step, slot, n] = y * (2 * SU) + x
                counts_ref[step, slot] = n + 1
                return i + 1

            lax.while_loop(more, put, jnp.int32(0))


def bucket(core, own, other):
    smem = pl.BlockSpec(memory_space=pltpu.SMEM)
    return pl.pallas_call(
        bucket_kernel,
        out_shape=(
            jax.ShapeDtypeStruct((STEPS, SU + 1, 2 * NPAIR), jnp.int32),
            jax.ShapeDtypeStruct((STEPS, 16), jnp.int32),
        ),
        in_specs=[smem, smem, smem],
        out_specs=(smem, smem),
        cost_estimate=pl.CostEstimate(flops=4_000_000, bytes_accessed=60_000, transcendentals=0),
    )(core, own, other)


def product_kernel(step, first, *refs):
    if first:
        where_ref, codes_ref, counts_ref, left_ref, right_ref, out_ref, lhs, rhs, prod = refs
    else:
        where_ref, codes_ref, counts_ref, left_ref, right_ref, acc_ref, out_ref, lhs, rhs, prod = refs
    r = where_ref[0]
    j = where_ref[1]
    k = lax.rem(r + j + step, GRID)

    def load_left(flip):
        for x in range(SU):
            tile = left_ref[x]
            if flip:
                tile = tile.T
            high = tile.astype(jnp.bfloat16)
            low = (tile - high.astype(jnp.float32)).astype(jnp.bfloat16)
            rows = slice(x * BS, (x + 1) * BS)
            lhs[rows, 0:BS] = high
            lhs[rows, BS : 2 * BS] = high
            lhs[rows, 2 * BS : 3 * BS] = low

    def load_right(flip):
        for y in range(SU):
            tile = right_ref[y]
            if flip:
                tile = tile.T
            high = tile.astype(jnp.bfloat16)
            low = (tile - high.astype(jnp.float32)).astype(jnp.bfloat16)
            cols = slice(y * BS, (y + 1) * BS)
            rhs[0:BS, cols] = high
            rhs[BS : 2 * BS, cols] = low
            rhs[2 * BS : 3 * BS, cols] = high

    def multiply(v, w):
        for yp in range(SU // 2):
            b = rhs[:, yp * 2 * BS : (yp + 1) * 2 * BS]
            for xp in range(SU // 2):
                a = lhs[xp * 2 * BS : (xp + 1) * 2 * BS, :]
                res = jnp.dot(a, b, preferred_element_type=jnp.float32)
                rows = slice((v * SU + 2 * xp) * BS, (v * SU + 2 * xp + 2) * BS)
                prod[w * SU + 2 * yp, rows, :] = res[:, :BS]
                prod[w * SU + 2 * yp + 1, rows, :] = res[:, BS:]

    def left_needed(v):
        return r <= k if v == 0 else r >= k

    def right_needed(w):
        return k <= j if w == 0 else k >= j

    for v in (0, 1):

        @pl.when(left_needed(v))
        def _(v=v):
            load_left(v == 1)
            for w in (0, 1):

                @pl.when(right_needed(w))
                def _(v=v, w=w):
                    load_right(w == 1)
                    multiply(v, w)

    for t in range(SU):
        if first:
            acc = jnp.zeros((BS, BS), jnp.float32)
        else:
            acc = acc_ref[t]

        def add(i, acc, t=t):
            code = codes_ref[step, t, i]
            y = code // (2 * SU)
            x = lax.rem(code, 2 * SU)
            return acc + prod[y, pl.ds(pl.multiple_of(x * BS, BS), BS), :]

        out_ref[t] = lax.fori_loop(0, counts_ref[step, t], add, acc)


def product(step, where, codes, counts, left, right, acc):
    smem = pl.BlockSpec(memory_space=pltpu.SMEM)
    vmem = pl.BlockSpec(memory_space=pltpu.VMEM)
    first = acc is None

    def kernel(*refs):
        product_kernel(step, first, *refs)

    args = (where, codes, counts, left, right) + (() if first else (acc,))
    return pl.pallas_call(
        kernel,
        out_shape=jax.ShapeDtypeStruct((SU, BS, BS), jnp.float32),
        in_specs=[smem, smem, smem, vmem, vmem] + ([] if first else [vmem]),
        out_specs=vmem,
        scratch_shapes=[
            pltpu.VMEM((SU * BS, 3 * BS), jnp.bfloat16),
            pltpu.VMEM((3 * BS, SU * BS), jnp.bfloat16),
            pltpu.VMEM((2 * SU, 2 * SU * BS, BS), jnp.float32),
        ],
        compiler_params=pltpu.CompilerParams(vmem_limit_bytes=32 * 1024 * 1024),
        cost_estimate=pl.CostEstimate(flops=3_000_000_000, bytes_accessed=1_500_000, transcendentals=0),
    )(*args)


def on_device(stored, pair_lists):
    r = lax.axis_index("row")
    c = lax.axis_index("col")
    j = c // 2
    core = c % 2
    mine = stored[0, 0]
    lists = pair_lists[0, 0]

    partner = lax.ppermute(mine, AXES, init_route())
    home = jnp.where((core == 0) == (r <= j), mine, partner)
    got0 = lax.ppermute(home, AXES, route(0))
    other_lists = lax.ppermute(lists, AXES, swap_route())
    codes, counts = bucket(core.astype(jnp.int32)[None], lists, other_lists)
    right_side = core == 1
    send1 = jnp.where(right_side, got0, home)
    got1 = lax.ppermute(send1, AXES, route(1))
    low = r < 8
    middle = (j % 8 == 3) | (j % 8 == 7)
    send2 = jnp.where(right_side, jnp.where(middle, got0, got1), got0)
    got2 = lax.ppermute(send2, AXES, route(2))
    swaps = [lax.ppermute(g, AXES, swap_route()) for g in (got0, got1, got2)]
    gots = [got0, got1, got2]

    lefts = [jnp.where(right_side, s, g) for s, g in zip(swaps, gots)]
    rights = [jnp.where(right_side, g, s) for s, g in zip(swaps, gots)]
    left = [
        jnp.where(low, lefts[0], lefts[1]),
        lefts[2],
        jnp.where(low, lefts[1], lefts[0]),
    ]
    up = j % 8 <= 2
    even = r % 2 == 0
    right = [
        jnp.where(middle, jnp.where(even, rights[2], rights[1]), jnp.where(up, rights[0], rights[2])),
        jnp.where(middle, rights[0], rights[1]),
        jnp.where(middle, jnp.where(even, rights[1], rights[2]), jnp.where(up, rights[2], rights[0])),
    ]
    where = jnp.stack([r, j]).astype(jnp.int32)
    acc = None
    for step in range(STEPS):
        acc = product(step, where, codes, counts, left[step], right[step], acc)
    return acc[None, None]


def solution(mesh):
    return jax.shard_map(
        on_device,
        mesh=mesh,
        in_specs=(P("row", "col", None, None, None), P("row", "col", None, None, None)),
        out_specs=P("row", "col", None, None, None),
        check_vma=False,
    )
```

```python
import jax
import jax.numpy as jnp
from jax import lax
from jax.experimental import pallas as pl
from jax.experimental.pallas import tpu as pltpu
from jax.sharding import PartitionSpec as P

STEPS = 3
GRID = 16
SU = 8
BS = 128
NPAIR = 128
AXES = ("row", "col")
CHUNK = 4
UNROLL = 2


def device(r, j, core):
    return (r * GRID + j) * 2 + core


def data_core(a, b):
    return 0 if a <= b else 1


def left_route(step, to_core):
    return [
        (device(r, (r + j + step) % GRID, data_core(r, (r + j + step) % GRID)), device(r, j, to_core))
        for r in range(GRID)
        for j in range(GRID)
    ]


def right_route(step, to_core):
    return [
        (device((r + j + step) % GRID, j, data_core((r + j + step) % GRID, j)), device(r, j, to_core))
        for r in range(GRID)
        for j in range(GRID)
    ]


def near_route(shift, to_core):
    return [(device((r + shift) % GRID, j, 1), device(r, j, to_core)) for r in range(GRID) for j in range(GRID)]


def swap_route():
    return [(d, d ^ 1) for d in range(2 * GRID * GRID)]


def bucket_kernel(core_ref, own_ref, other_ref, codes_ref, counts_ref):
    core = core_ref[0]
    groups = ((1, 2 * SU), (2 * core, 2 * SU))
    for group, (_, slots) in enumerate(groups):
        for t in range(slots + 1):
            counts_ref[group, t] = 0
    for ref in (own_ref, other_ref):

        def more(i, ref=ref):
            at = jnp.minimum(i, NPAIR - CHUNK)
            real = jnp.logical_or(ref[groups[0][0], 2, at] < 2 * SU, ref[groups[1][0], 2, at] < 2 * SU)
            return jnp.logical_and(i < NPAIR, real)

        def put(i, ref=ref):
            for n in range(CHUNK):
                for group, (step, slots) in enumerate(groups):
                    x = jnp.minimum(ref[step, 0, i + n], 2 * SU - 1)
                    y = jnp.minimum(ref[step, 1, i + n], 2 * SU - 1)
                    t = ref[step, 2, i + n]
                    slot = jnp.where(t < 2 * SU, jnp.bitwise_xor(t, core * SU), 2 * SU)
                    slot = jnp.minimum(slot, slots)
                    m = counts_ref[group, slot]
                    codes_ref[group, slot, m] = y * (2 * SU) + x
                    counts_ref[group, slot] = m + 1
            return i + CHUNK

        lax.while_loop(more, put, jnp.int32(0))
    for group, (_, slots) in enumerate(groups):
        for t in range(slots):
            m = counts_ref[group, t]
            for n in range(UNROLL - 1):
                codes_ref[group, t, m + n] = 4 * SU * SU
            counts_ref[group, t] = (m + UNROLL - 1) // UNROLL


def bucket(core, own, other):
    smem = pl.BlockSpec(memory_space=pltpu.SMEM)
    return pl.pallas_call(
        bucket_kernel,
        out_shape=(
            jax.ShapeDtypeStruct((2, 2 * SU + 1, 2 * NPAIR + 128), jnp.int32),
            jax.ShapeDtypeStruct((2, 2 * SU + 1), jnp.int32),
        ),
        in_specs=[smem, smem, smem],
        out_specs=(smem, smem),
        cost_estimate=pl.CostEstimate(flops=1000, bytes_accessed=1000, transcendentals=0),
    )(core, own, other)


def product_kernel(group, where_ref, codes_ref, counts_ref, left_ref, right_ref, *refs):
    if group == 0:
        out_ref, lhs, rhs, prod = refs
    else:
        acc_ref, own_ref, sent_ref, lhs, rhs, prod = refs
    r = where_ref[0]
    j = where_ref[1]
    core = where_ref[2]
    k = lax.rem(r + j + (1 if group == 0 else 2 * core), GRID)

    def halves(tile):
        high = tile.astype(jnp.bfloat16)
        return high, (tile - high.astype(jnp.float32)).astype(jnp.bfloat16)

    def load_left(flip):
        for x in range(SU):
            high, low = halves(left_ref[x].T if flip else left_ref[x])
            rows = slice(x * BS, (x + 1) * BS)
            lhs[rows, 0:BS] = high
            lhs[rows, BS : 2 * BS] = high
            lhs[rows, 2 * BS : 3 * BS] = low

    def load_right(flip):
        for y in range(SU):
            high, low = halves(right_ref[y].T if flip else right_ref[y])
            cols = slice(y * BS, (y + 1) * BS)
            rhs[0:BS, cols] = high
            rhs[BS : 2 * BS, cols] = low
            rhs[2 * BS : 3 * BS, cols] = high

    def multiply(v, w):
        for yp in range(SU // 2):
            b = rhs[:, yp * 2 * BS : (yp + 1) * 2 * BS]
            for xp in range(SU // 2):
                a = lhs[xp * 2 * BS : (xp + 1) * 2 * BS, :]
                res = jnp.dot(a, b, preferred_element_type=jnp.float32)
                rows = slice((v * SU + 2 * xp) * BS, (v * SU + 2 * xp + 2) * BS)
                prod[w * SU + 2 * yp, rows, :] = res[:, :BS]
                prod[w * SU + 2 * yp + 1, rows, :] = res[:, BS:]

    def make_products():
        prod[2 * SU, 0:BS, :] = jnp.zeros((BS, BS), jnp.float32)
        for v in (0, 1):

            @pl.when(r <= k if v == 0 else r >= k)
            def _(v=v):
                load_left(v == 1)
                for w in (0, 1):

                    @pl.when(k <= j if w == 0 else k >= j)
                    def _(v=v, w=w):
                        load_right(w == 1)
                        multiply(v, w)

    def total(t, acc):
        def add(i, acc):
            for n in range(UNROLL):
                code = codes_ref[group, t, UNROLL * i + n]
                y = lax.shift_right_logical(code, 4)
                x = jnp.bitwise_and(code, 15)
                acc = acc + prod[y, pl.ds(pl.multiple_of(x * BS, BS), BS), :]
            return acc

        return lax.fori_loop(0, counts_ref[group, t], add, acc)

    if group == 0:

        @pl.when(core == 0)
        def _():
            out_ref[...] = jnp.zeros_like(out_ref)

        @pl.when(core == 1)
        def _():
            make_products()
            for t in range(2 * SU):
                out_ref[t] = total(t, jnp.zeros((BS, BS), jnp.float32))

    else:
        make_products()
        for t in range(SU):
            own_ref[t] = total(t, acc_ref[t])
        for t in range(SU):
            sent_ref[t] = total(SU + t, acc_ref[SU + t])


def product(group, where, codes, counts, left, right, acc):
    smem = pl.BlockSpec(memory_space=pltpu.SMEM)
    vmem = pl.BlockSpec(memory_space=pltpu.VMEM)
    tiles = jax.ShapeDtypeStruct((SU, BS, BS), jnp.float32)

    def kernel(*refs):
        product_kernel(group, *refs)

    args = (where, codes, counts, left, right) + (() if group == 0 else (acc,))
    return pl.pallas_call(
        kernel,
        out_shape=jax.ShapeDtypeStruct((2 * SU, BS, BS), jnp.float32) if group == 0 else (tiles, tiles),
        in_specs=[smem, smem, smem, vmem, vmem] + [vmem] * group,
        out_specs=vmem if group == 0 else (vmem, vmem),
        scratch_shapes=[
            pltpu.VMEM((SU * BS, 3 * BS), jnp.bfloat16),
            pltpu.VMEM((3 * BS, SU * BS), jnp.bfloat16),
            pltpu.VMEM((2 * SU + 1, 2 * SU * BS, BS), jnp.float32),
        ],
        compiler_params=pltpu.CompilerParams(vmem_limit_bytes=32 * 1024 * 1024),
        cost_estimate=pl.CostEstimate(flops=1000, bytes_accessed=1000, transcendentals=0),
    )(*args)


def on_device(stored, pair_lists):
    r = lax.axis_index("row")
    c = lax.axis_index("col")
    j = c // 2
    core = c % 2
    mine = stored[0, 0]
    lists = pair_lists[0, 0]
    low = core == 0

    middle = lax.ppermute(mine, AXES, right_route(1, 1))
    left1 = lax.ppermute(mine, AXES, left_route(1, 1))
    left0 = lax.ppermute(mine, AXES, left_route(0, 0))
    left2 = lax.ppermute(mine, AXES, left_route(2, 1))
    right0 = lax.ppermute(middle, AXES, near_route(-1, 0))
    right2 = lax.ppermute(middle, AXES, near_route(1, 1))

    other_lists = lax.ppermute(lists, AXES, swap_route())
    codes, counts = bucket(core.astype(jnp.int32)[None], lists, other_lists)
    where = jnp.stack([r, j, core]).astype(jnp.int32)
    acc = product(0, where, codes, counts, left1, middle, None)
    kept, sent = product(
        1, where, codes, counts, jnp.where(low, left0, left2), jnp.where(low, right0, right2), acc
    )
    return (kept + lax.ppermute(sent, AXES, swap_route()))[None, None]


def solution(mesh):
    return jax.shard_map(
        on_device,
        mesh=mesh,
        in_specs=(P("row", "col", None, None, None), P("row", "col", None, None, None)),
        out_specs=P("row", "col", None, None, None),
        check_vma=False,
    )
```

```python
import jax
import jax.numpy as jnp
from jax import lax
from jax.experimental import pallas as pl
from jax.experimental.pallas import tpu as pltpu
from jax.sharding import PartitionSpec as P

STEPS = 3
GRID = 16
SU = 8
BS = 128
NPAIR = 128
AXES = ("row", "col")


def device(r, j, core):
    return (r * GRID + j) * 2 + core


def data_core(a, b):
    return 0 if a <= b else 1


def left_route(step, to_core):
    return [
        (device(r, (r + j + step) % GRID, data_core(r, (r + j + step) % GRID)), device(r, j, to_core))
        for r in range(GRID)
        for j in range(GRID)
    ]


def right_route(step, to_core):
    return [
        (device((r + j + step) % GRID, j, data_core((r + j + step) % GRID, j)), device(r, j, to_core))
        for r in range(GRID)
        for j in range(GRID)
    ]


def near_route(shift, to_core):
    return [(device((r + shift) % GRID, j, 1), device(r, j, to_core)) for r in range(GRID) for j in range(GRID)]


def swap_route():
    return [(d, d ^ 1) for d in range(2 * GRID * GRID)]


def product_kernel(group, where_ref, lists_ref, *refs):
    if group == 0:
        left_in, right_in, acc_ref = refs[:3]
        sources = (None, (left_in, right_in))
    else:
        left0, left2, right0, right2, acc_ref, kept_ref, sent_ref = refs[:7]
        sources = ((left0, right0), (left2, right2))
    left_ref, right_ref, sems, lhs, rhs, prod, even_ref, odd_ref = refs[-8:]
    r = where_ref[0]
    j = where_ref[1]
    core = where_ref[2]
    step = 1 if group == 0 else 2 * core
    k = lax.rem(r + j + step, GRID)

    def halves(tile):
        high = tile.astype(jnp.bfloat16)
        return high, (tile - high.astype(jnp.float32)).astype(jnp.bfloat16)

    def load_left(flip):
        for x in range(SU):
            high, low = halves(left_ref[x].T if flip else left_ref[x])
            rows = slice(x * BS, (x + 1) * BS)
            lhs[rows, 0:BS] = high
            lhs[rows, BS : 2 * BS] = high
            lhs[rows, 2 * BS : 3 * BS] = low

    def load_right(flip):
        for y in range(SU):
            high, low = halves(right_ref[y].T if flip else right_ref[y])
            cols = slice(y * BS, (y + 1) * BS)
            rhs[0:BS, cols] = high
            rhs[BS : 2 * BS, cols] = low
            rhs[2 * BS : 3 * BS, cols] = high

    def multiply(v, w):
        for yp in range(SU // 2):
            b = rhs[:, yp * 2 * BS : (yp + 1) * 2 * BS]
            for xp in range(SU // 2):
                a = lhs[xp * 2 * BS : (xp + 1) * 2 * BS, :]
                res = jnp.dot(a, b, preferred_element_type=jnp.float32)
                rows = pl.ds(pl.multiple_of((v * SU + 2 * xp) * BS, BS), 2 * BS)
                prod[w * SU + 2 * yp, rows, :] = res[:, :BS]
                prod[w * SU + 2 * yp + 1, rows, :] = res[:, BS:]

    def copies(side):
        pair = sources[side]
        return [pltpu.make_async_copy(pair[n], (left_ref, right_ref)[n], sems.at[n]) for n in range(2)]

    def make_products():
        @pl.when(r <= k)
        def _():
            load_left(False)

        @pl.when(r > k)
        def _():
            load_left(True)

        copies(1)[1].wait()

        @pl.when(k <= j)
        def _():
            load_right(False)

        @pl.when(k > j)
        def _():
            load_right(True)

        v = (r > k).astype(jnp.int32)
        w = (k > j).astype(jnp.int32)
        multiply(v, w)

        @pl.when(r == k)
        def _():
            load_left(True)
            multiply(1, w)

        @pl.when(k == j)
        def _():
            load_right(True)
            multiply(jnp.where(r == k, 1, v), 1)

            @pl.when(r == k)
            def _():
                load_left(False)
                multiply(0, 1)

    def add_products(side):
        ref = lists_ref.at[side]
        count = jnp.int32(0)
        jump = NPAIR
        while jump:
            at = jnp.minimum(count + jump, NPAIR) - 1
            real = jnp.logical_and(count + jump <= NPAIR, ref[step, 2, at] < 2 * SU)
            count = jnp.where(real, count + jump, count)
            jump //= 2

        def add(i, acc):
            x = jnp.minimum(ref[step, 0, i], 2 * SU - 1)
            y = jnp.minimum(ref[step, 1, i], 2 * SU - 1)
            t = jnp.bitwise_xor(ref[step, 2, i], core * SU)
            acc[t] = acc[t] + prod[y, pl.ds(pl.multiple_of(x * BS, BS), BS), :]

        def four(i, carry):
            for n in range(4):
                add(4 * i + n, (even_ref, odd_ref)[n % 2])
            return carry

        def one(i, carry):
            add(i, even_ref)
            return carry

        lax.fori_loop(0, count // 4, four, 0)
        lax.fori_loop(count - count % 4, count, one, 0)

    def run():
        even_ref[...] = jnp.zeros_like(even_ref)
        odd_ref[...] = jnp.zeros_like(odd_ref)
        copies(1)[0].wait()
        make_products()
        add_products(0)
        add_products(1)

    for side in range(2):
        if sources[side] is not None:

            @pl.when(core == side)
            def _(side=side):
                for copy in copies(side):
                    copy.start()

    if group == 0:

        @pl.when(core == 0)
        def _():
            acc_ref[...] = jnp.zeros_like(acc_ref)

        @pl.when(core == 1)
        def _():
            run()
            for t in range(2 * SU):
                acc_ref[t] = even_ref[t] + odd_ref[t]

    else:
        run()
        for t in range(SU):
            sent_ref[t] = even_ref[SU + t] + odd_ref[SU + t] + acc_ref[SU + t]
        for t in range(SU):
            kept_ref[t] = even_ref[t] + odd_ref[t] + acc_ref[t]


def product(group, where, lists, panels, acc):
    smem = pl.BlockSpec(memory_space=pltpu.SMEM)
    vmem = pl.BlockSpec(memory_space=pltpu.VMEM)
    hbm = pl.BlockSpec(memory_space=pl.ANY)
    out = jax.ShapeDtypeStruct(((2 - group) * SU, BS, BS), jnp.float32)

    def kernel(*refs):
        product_kernel(group, *refs)

    return pl.pallas_call(
        kernel,
        out_shape=(out,) * (1 + group),
        in_specs=[smem] * 2 + [hbm] * len(panels) + [vmem] * len(acc),
        out_specs=(vmem,) * (1 + group),
        scratch_shapes=[
            pltpu.VMEM((SU, BS, BS), jnp.float32),
            pltpu.VMEM((SU, BS, BS), jnp.float32),
            pltpu.SemaphoreType.DMA((2,)),
            pltpu.VMEM((SU * BS, 3 * BS), jnp.bfloat16),
            pltpu.VMEM((3 * BS, SU * BS), jnp.bfloat16),
            pltpu.VMEM((2 * SU, 2 * SU * BS, BS), jnp.float32),
            pltpu.VMEM((2 * SU, BS, BS), jnp.float32),
            pltpu.VMEM((2 * SU, BS, BS), jnp.float32),
        ],
        compiler_params=pltpu.CompilerParams(vmem_limit_bytes=36 * 1024 * 1024),
        cost_estimate=pl.CostEstimate(flops=1000, bytes_accessed=1000, transcendentals=0),
    )(where, lists, *panels, *acc)


def on_device(stored, pair_lists):
    r = lax.axis_index("row")
    c = lax.axis_index("col")
    j = c // 2
    core = c % 2
    mine = stored[0, 0]
    lists = pair_lists[0, 0]

    middle = lax.ppermute(mine, AXES, right_route(1, 1))
    left1 = lax.ppermute(mine, AXES, left_route(1, 1))
    left0 = lax.ppermute(mine, AXES, left_route(0, 0))
    left2 = lax.ppermute(mine, AXES, left_route(2, 1))
    right0 = lax.ppermute(middle, AXES, near_route(-1, 0))
    right2 = lax.ppermute(middle, AXES, near_route(1, 1))

    both = jnp.stack([lists, lax.ppermute(lists, AXES, swap_route())])
    where = jnp.stack([r, j, core]).astype(jnp.int32)
    acc = product(0, where, both, (left1, middle), ())
    kept, sent = product(1, where, both, (left0, left2, right0, right2), acc)
    return (kept + lax.ppermute(sent, AXES, swap_route()))[None, None]


def solution(mesh):
    return jax.shard_map(
        on_device,
        mesh=mesh,
        in_specs=(P("row", "col", None, None, None), P("row", "col", None, None, None)),
        out_specs=P("row", "col", None, None, None),
        check_vma=False,
    )
```
